32 devices in a mesh: prow: 8 (over z, x), pcol: 4 (over y, core).
Axes of the slice: x: 2, y: 2, z: 4, core: 2. Of those that a mesh axis runs over, the one named last changes fastest.
Arguments:
- sigma_top: bfloat16 [8192, 8192], P('prow', 'pcol'), may hold values from -400 to 400, as said below
- panel_par: bfloat16 [8192, 1024], P('prow', 'pcol'), may hold values from -0.119628906 to 0.119628906
- panel_kid: bfloat16 [8192, 2048], P('prow', 'pcol'), may hold values from -0.119628906 to 0.119628906
- link_kid: bfloat16 [8, 256, 256], P('pcol'), may hold values from -0.23925781 to 0.23925781
- dinv_par: float32 [4, 256, 256], P('pcol'), may hold values from -6 to 6
- dinv_kid: float32 [8, 256, 256], P('pcol'), may hold values from -6 to 6
- mask_par: int32 [4, 32], P('pcol', 'prow'), may hold values 0 or 1
- mask_kid: int32 [8, 32], P('pcol', 'prow'), may hold values 0 or 1
Outputs:
- sigma_par: bfloat16 [8192, 1024], P('prow', 'pcol')
- diag_par: float32 [4, 256, 256], P('pcol')
- sigma_kid: bfloat16 [8192, 2048], P('prow', 'pcol')
- link_sigma: float32 [8, 256, 256], P('pcol')
- diag_kid: float32 [8, 256, 256], P('pcol')
The draws below stay inside these ranges and needn't reach their ends.
Inputs may be any that keep to these rules, and one draw needn't show every extreme that they name: `sigma_top`: symmetric.
All inputs are finite; a program needn't handle non-finite values. No bound on the sum of `mask_par` or of `mask_kid` on one device may be relied on, other than what follows from the above.
Results may differ from the reference program's by a relative error of at most 0.015.
Values may be sent and summed in bfloat16 or wider, within the bound.
A program may use at most 64 MiB of HBM per device.

```python
import jax
import jax.numpy as jnp
from jax import lax

WIDTH = 256
ANC = 32
KIDS = 2
PARENTS = 4
CHILDREN = 8
ORDER = 8192


def draw_sigma_top(key, part):
    order_total = ANC * WIDTH
    noise = jax.random.normal(jax.random.fold_in(key, 11), (order_total, order_total), jnp.float32)
    symmetric = (noise + noise.T) * 0.7071067811865476
    index = jnp.arange(order_total)
    eye = (index[:, None] == index[None, :]).astype(jnp.float32)
    base = 8.0 * (symmetric / jnp.sqrt(jnp.float32(order_total)) + 3.0 * eye)
    return base.astype(jnp.bfloat16)


def plant(drawn, rng, smallest, top_value):
    spot = [jax.random.randint(jax.random.fold_in(rng, axis), (), 0, length) for axis, length in enumerate(drawn.shape)]
    main_axis = drawn.shape.index(max(drawn.shape))
    beside = spot[:main_axis] + [(spot[main_axis] + 1) % drawn.shape[main_axis]] + spot[main_axis + 1:]
    return drawn.at[tuple(spot)].set(smallest).at[tuple(beside)].set(top_value)


def steps_of(key, extent, cuts, smallest, high):
    level = 1.0
    for position, shards_of in cuts:
        steps = jax.random.uniform(jax.random.fold_in(jax.random.fold_in(key, 6), position), (shards_of,), jnp.float32, smallest / len(cuts), high / len(cuts))
        level = level * jnp.repeat(jnp.exp(steps), extent[position] // shards_of).reshape((-1,) + (1,) * (len(extent) - 1 - position))
    return level


def normal_values(key, extent, scale, bound, cuts=(), held_as=jnp.bfloat16):
    array = scale * jax.random.normal(key, extent, jnp.float32)
    if cuts:
        array = array * steps_of(key, extent, cuts, -0.22, 0.18)
    return jnp.clip(array, -bound, bound).astype(held_as)


def setup_inputs(seed: int = 0) -> dict:
    key_of = jax.random.split(jax.random.key(seed), 9)
    sigma_top = draw_sigma_top(jax.random.fold_in(key_of[8], 71), 0)
    panel_par = normal_values(key_of[1], (ORDER, PARENTS * WIDTH), 0.02, 0.119628906, ((0, 8), (1, 4)))
    panel_kid = normal_values(key_of[2], (ORDER, CHILDREN * WIDTH), 0.02, 0.119628906, ((0, 8), (1, 4)))
    link_kid = normal_values(key_of[3], (CHILDREN, WIDTH, WIDTH), 0.04, 0.23925781, ((0, 4),))
    dinv_par = normal_values(key_of[4], (PARENTS, WIDTH, WIDTH), 1.0, 6.0, ((0, 4),), jnp.float32)
    dinv_kid = normal_values(key_of[5], (CHILDREN, WIDTH, WIDTH), 1.0, 6.0, ((0, 4),), jnp.float32)
    mask_par = plant((jax.random.randint(key_of[6], (PARENTS, ANC), 0, 2) < 1).astype(jnp.int32), jax.random.fold_in(key_of[6], 1), 0, 1)
    mask_kid = plant((jax.random.randint(key_of[7], (CHILDREN, ANC), 0, 2) < 1).astype(jnp.int32), jax.random.fold_in(key_of[7], 1), 0, 1)
    return dict(sigma_top=sigma_top, panel_par=panel_par, panel_kid=panel_kid, link_kid=link_kid, dinv_par=dinv_par, dinv_kid=dinv_kid, mask_par=mask_par, mask_kid=mask_kid)


def expand_rows(mask, width):
    count, blocks = mask.shape
    spread = jnp.broadcast_to(mask.T.astype(jnp.float32)[:, None, :, None], (blocks, width, count, width))
    return spread.reshape(blocks * width, count * width)


def reference(sigma_top, panel_par, panel_kid, link_kid, dinv_par, dinv_kid, mask_par, mask_kid):
    highest = lax.Precision.HIGHEST
    kid_pattern = mask_kid * jnp.repeat(mask_par, KIDS, axis=0)
    par_rows = expand_rows(mask_par, WIDTH)
    kid_rows = expand_rows(kid_pattern, WIDTH)
    low_par = panel_par.astype(jnp.float32) * par_rows
    low_kid = panel_kid.astype(jnp.float32) * kid_rows
    sigma_full = sigma_top.astype(jnp.float32)
    prod_par = jnp.dot(sigma_full, low_par, precision=highest)
    sigma_par = (-prod_par * par_rows).astype(jnp.bfloat16)
    par_blocks = sigma_par.astype(jnp.float32).reshape(ORDER, PARENTS, WIDTH)
    par_spread = jnp.repeat(par_blocks, KIDS, axis=1)
    link_wide = link_kid.astype(jnp.float32)
    carried = jnp.einsum('rcb,cbd->rcd', par_spread, link_wide, precision=highest)
    prod_kid = jnp.dot(sigma_full, low_kid, precision=highest)
    sigma_kid = (-(prod_kid + carried.reshape(ORDER, CHILDREN * WIDTH)) * kid_rows).astype(jnp.bfloat16)
    low_par3 = low_par.reshape(ORDER, PARENTS, WIDTH)
    low_kid3 = low_kid.reshape(ORDER, CHILDREN, WIDTH)
    kid_blocks = sigma_kid.astype(jnp.float32).reshape(ORDER, CHILDREN, WIDTH)
    diag_par = dinv_par - jnp.einsum('rpb,rpd->pbd', low_par3, par_blocks, precision=highest)
    cross = jnp.einsum('rcb,rcd->cbd', par_spread, low_kid3, precision=highest)
    diag_spread = jnp.repeat(diag_par, KIDS, axis=0)
    link_sigma = -(cross + jnp.einsum('cab,cbd->cad', diag_spread, link_wide, precision=highest))
    diag_kid = dinv_kid - jnp.einsum('rcb,rcd->cbd', low_kid3, kid_blocks, precision=highest)
    diag_kid = diag_kid - jnp.einsum('cba,cbd->cad', link_wide, link_sigma, precision=highest)
    return sigma_par, diag_par, sigma_kid, link_sigma, diag_kid
```

```python
import functools

import jax
import jax.numpy as jnp
from jax import lax
from jax.experimental import pallas as pl
from jax.experimental.pallas import tpu as pltpu
from jax.sharding import PartitionSpec as P

KIDS = 2
PIECES = 4
MESH = pl.DeviceIdType.MESH


def gather_kernel(line, chips, tile_ref, low_ref, sig_ref, all_ref, s_self, y_send, y_recv, c_send,
                  c_recv, z_send, z_recv, x_send, x_recv):
    row = lax.axis_index("prow")
    col = lax.axis_index("pcol")
    place, side = row // 2, row % 2
    chip, core = col // 2, col % 2
    height, width = tile_ref.shape
    depth = low_ref.shape[0]
    after, before = (place + 1) % line, (place + line - 1) % line
    dev_x = (place * 2 + 1 - side, col)
    dev_up = (after * 2 + side, col)
    dev_down = (before * 2 + side, col)
    dev_core = (row, chip * 2 + 1 - core)
    dev_y = [(row, (chip + d) % chips * 2 + core) for d in range(1, chips)]

    barrier = pltpu.get_barrier_semaphore()
    for dev in [dev_x, dev_up, dev_down, dev_core] + dev_y:
        pl.semaphore_signal(barrier, inc=1, device_id=dev, device_id_type=MESH)
    pl.semaphore_wait(barrier, 4 + len(dev_y))

    hs = height // PIECES
    ds = depth // PIECES

    def sig_at(owner, s):
        start = pl.multiple_of(owner * width, width)
        return sig_ref.at[pl.ds(s * hs, hs), pl.ds(start, width)]

    def low_at(block, s):
        start = pl.multiple_of(block * depth + s * ds, ds)
        return all_ref.at[pl.ds(start, ds), :]

    def remote(src, dst, send, recv, dev):
        return pltpu.make_async_remote_copy(src_ref=src, dst_ref=dst, send_sem=send,
                                            recv_sem=recv, device_id=dev, device_id_type=MESH)

    def tile_piece(s):
        return tile_ref.at[pl.ds(s * hs, hs), :]

    def low_piece(s):
        return low_ref.at[pl.ds(s * ds, ds), :]

    def to_x(slot, block, s, src):
        return remote(src, low_at(block, s), x_send.at[slot, s], x_recv.at[slot, s], dev_x)

    def to_z(way, t, block, s, src):
        return remote(src, low_at(block, s), z_send.at[way, t, s], z_recv.at[way, t, s],
                      dev_up if way == 0 else dev_down)

    def to_y(d, s):
        return remote(tile_piece(s), sig_at(col, s), y_send.at[d - 1, s], y_recv.at[d - 1, s],
                      dev_y[d - 1])

    def to_core(d, s, owner, src):
        return remote(src, sig_at(owner, s), c_send.at[d, s], c_recv.at[d, s], dev_core)

    can_up = place < line - 1
    can_down = place > 0
    for s in range(PIECES):
        pl.when(can_up)(lambda: to_z(0, 0, row, s, low_piece(s)).start())
        pl.when(can_down)(lambda: to_z(1, 0, row, s, low_piece(s)).start())
        to_x(0, row, s, low_piece(s)).start()
        for d in range(1, chips):
            to_y(d, s).start()
        to_core(0, s, col, tile_piece(s)).start()
    own_sig = pltpu.make_async_copy(
        tile_ref, sig_ref.at[:, pl.ds(pl.multiple_of(col * width, width), width)], s_self.at[0])
    own_low = pltpu.make_async_copy(
        low_ref, all_ref.at[pl.ds(pl.multiple_of(row * depth, depth), depth), :], s_self.at[1])
    own_sig.start()
    own_low.start()

    def from_line(way, t):
        block = row - 2 * t if way == 0 else row + 2 * t
        here = place - t >= 0 if way == 0 else place + t < line
        onward = (here & can_up) if way == 0 else (here & can_down)
        slot = t if way == 0 else line - 1 + t
        return block, here, onward, slot

    def pass_low(way, t, s):
        block, here, onward, slot = from_line(way, t)

        @pl.when(here)
        def _():
            to_z(way, t - 1, block, s, low_at(block, s)).wait_recv()
            to_x(slot, block, s, low_at(block, s)).start()
        if t < line - 1:
            @pl.when(onward)
            def _():
                to_z(way, t, block, s, low_at(block, s)).start()

    def pass_sig(d, s):
        owner = (chip + chips - d) % chips * 2 + core
        to_y(d, s).wait_recv()
        to_core(d, s, owner, sig_at(owner, s)).start()

    lows = [(t, s) for t in range(1, line) for s in range(PIECES)]
    sigs = [(d, s) for s in range(PIECES) for d in range(1, chips)]
    done = 0
    for i, (t, s) in enumerate(lows):
        pass_low(0, t, s)
        pass_low(1, t, s)
        upto = (i + 1) * len(sigs) // len(lows)
        for d, p in sigs[done:upto]:
            pass_sig(d, p)
        done = upto

    for s in range(PIECES):
        to_x(0, row, s, low_piece(s)).wait()
        for d in range(chips):
            to_core(d, s, col, tile_piece(s)).wait()
        for d in range(1, chips):
            to_y(d, s).wait_send()
        pl.when(can_up)(lambda: to_z(0, 0, row, s, low_piece(s)).wait_send())
        pl.when(can_down)(lambda: to_z(1, 0, row, s, low_piece(s)).wait_send())
        for t in range(1, line):
            for way in range(2):
                block, here, onward, slot = from_line(way, t)

                @pl.when(here)
                def _():
                    to_x(slot, block, s, low_at(block, s)).wait()
                if t < line - 1:
                    @pl.when(onward)
                    def _():
                        to_z(way, t, block, s, low_at(block, s)).wait_send()
    own_sig.wait()
    own_low.wait()


def gather_all(rows, cols, tile, low):
    line, chips = rows // 2, cols // 2
    height, width = tile.shape
    depth, count = low.shape
    dma = pltpu.SemaphoreType.DMA
    return pl.pallas_call(
        functools.partial(gather_kernel, line, chips),
        out_shape=(
            jax.ShapeDtypeStruct((height, cols * width), tile.dtype),
            jax.ShapeDtypeStruct((rows * depth, count), low.dtype),
        ),
        in_specs=[pl.BlockSpec(memory_space=pl.ANY)] * 2,
        out_specs=[pl.BlockSpec(memory_space=pl.ANY)] * 2,
        scratch_shapes=[
            dma((2,)),
            dma((max(chips - 1, 1), PIECES)), dma((max(chips - 1, 1), PIECES)),
            dma((chips, PIECES)), dma((chips, PIECES)),
            dma((2, line, PIECES)), dma((2, line, PIECES)),
            dma((2 * line - 1, PIECES)), dma((2 * line - 1, PIECES)),
        ],
        compiler_params=pltpu.CompilerParams(collective_id=0, has_side_effects=True),
    )(tile, low)


def sum_kernel(count, part_ref, out_ref, got, s_send, s_recv, g_send, g_recv):
    row = lax.axis_index("prow")
    col = lax.axis_index("pcol")
    size = part_ref.shape[0] // count
    peers = [((row + d) % count, col) for d in range(1, count)]
    barrier = pltpu.get_barrier_semaphore()
    for dev in peers:
        pl.semaphore_signal(barrier, inc=1, device_id=dev, device_id_type=MESH)
    pl.semaphore_wait(barrier, len(peers))

    def share(block):
        return pl.ds(pl.multiple_of(block * size, size), size)

    def scatter(d):
        return pltpu.make_async_remote_copy(
            src_ref=part_ref.at[share((row + d) % count), :], dst_ref=got.at[d - 1],
            send_sem=s_send.at[d - 1], recv_sem=s_recv.at[d - 1], device_id=peers[d - 1],
            device_id_type=MESH)

    def spread(d):
        return pltpu.make_async_remote_copy(
            src_ref=out_ref.at[share(row), :], dst_ref=out_ref.at[share(row), :],
            send_sem=g_send.at[d - 1], recv_sem=g_recv.at[d - 1], device_id=peers[d - 1],
            device_id_type=MESH)

    for d in range(1, count):
        scatter(d).start()
    total = part_ref[share(row), :].astype(jnp.float32)
    for d in range(1, count):
        scatter(d).wait_recv()
        total = total + got[d - 1].astype(jnp.float32)
    out_ref[share(row), :] = total.astype(out_ref.dtype)
    for d in range(1, count):
        spread(d).start()
    for d in range(1, count):
        scatter(d).wait_send()
        spread(d).wait()


def sum_parts(count, parts):
    size = parts.shape[0] // count
    dma = pltpu.SemaphoreType.DMA
    return pl.pallas_call(
        functools.partial(sum_kernel, count),
        out_shape=jax.ShapeDtypeStruct(parts.shape, parts.dtype),
        in_specs=[pl.BlockSpec(memory_space=pltpu.VMEM)],
        out_specs=pl.BlockSpec(memory_space=pltpu.VMEM),
        scratch_shapes=[
            pltpu.VMEM((count - 1, size, parts.shape[1]), parts.dtype),
            dma((count - 1,)), dma((count - 1,)), dma((count - 1,)), dma((count - 1,)),
        ],
        compiler_params=pltpu.CompilerParams(collective_id=1, has_side_effects=True),
    )(parts)


def expand_rows(mask, width):
    count, blocks = mask.shape
    spread = jnp.broadcast_to(
        mask.T.astype(jnp.float32)[:, None, :, None], (blocks, width, count, width)
    )
    return spread.reshape(blocks * width, count * width)


def batch_mult(left, right):
    return jnp.einsum("cab,cbd->cad", left, right, precision=lax.Precision.HIGHEST)


def batch_tmult(left, right):
    return jnp.einsum("cba,cbd->cad", left, right, precision=lax.Precision.HIGHEST)


def on_device(rows, cols, sigma_top, panel_par, panel_kid, link_kid, dinv_par, dinv_kid, mask_par, mask_kid):
    width = dinv_par.shape[1]
    par_here = dinv_par.shape[0]
    kid_here = dinv_kid.shape[0]
    row_count = sigma_top.shape[0]
    kid_pattern = mask_kid * jnp.repeat(mask_par, KIDS, axis=0)
    par_rows = expand_rows(mask_par, width)
    kid_rows = expand_rows(kid_pattern, width)
    low_par = panel_par * par_rows.astype(jnp.bfloat16)
    low_kid = panel_kid * kid_rows.astype(jnp.bfloat16)
    low_all = jnp.concatenate([low_par, low_kid], axis=1)
    sigma_rows, low_rows = gather_all(rows, cols, sigma_top, low_all)
    prod = jnp.dot(sigma_rows, low_rows, preferred_element_type=jnp.float32)
    prod_par = prod[:, : par_here * width]
    prod_kid = prod[:, par_here * width :]
    sigma_par = (-prod_par * par_rows).astype(jnp.bfloat16)
    par_blocks = sigma_par.reshape(row_count, par_here, width)
    par_spread = jnp.repeat(par_blocks, KIDS, axis=1)
    carried = jnp.einsum("rcb,cbd->rcd", par_spread, link_kid, preferred_element_type=jnp.float32)
    sigma_kid = (-(prod_kid + carried.reshape(row_count, kid_here * width)) * kid_rows).astype(
        jnp.bfloat16
    )
    low_par3 = low_par.reshape(row_count, par_here, width)
    low_kid3 = low_kid.reshape(row_count, kid_here, width)
    kid_blocks = sigma_kid.reshape(row_count, kid_here, width)
    part_par = jnp.einsum("rpb,rpd->pbd", low_par3, par_blocks, preferred_element_type=jnp.float32)
    part_cross = jnp.einsum(
        "rcb,rcd->cbd", par_spread, low_kid3, preferred_element_type=jnp.float32
    )
    part_kid = jnp.einsum("rcb,rcd->cbd", low_kid3, kid_blocks, preferred_element_type=jnp.float32)
    link_wide = link_kid.astype(jnp.float32)
    parts = jnp.concatenate([part_par, part_cross, part_kid], axis=0).astype(jnp.bfloat16)
    total = sum_parts(rows, parts.reshape(-1, width)).astype(jnp.float32)
    total = total.reshape(parts.shape)
    sum_par = total[:par_here]
    cross_sum = total[par_here : par_here + kid_here]
    kid_sum = total[par_here + kid_here :]
    diag_par = dinv_par - sum_par
    diag_spread = jnp.repeat(diag_par, KIDS, axis=0)
    link_sigma = -(cross_sum + batch_mult(diag_spread, link_wide))
    diag_kid = dinv_kid - kid_sum - batch_tmult(link_wide, link_sigma)
    return (sigma_par, diag_par, sigma_kid, link_sigma, diag_kid)


def solution(mesh):
    placed = (
        P("prow", "pcol"),
        P("prow", "pcol"),
        P("prow", "pcol"),
        P("pcol", None, None),
        P("pcol", None, None),
        P("pcol", None, None),
        P("pcol", "prow"),
        P("pcol", "prow"),
    )
    return jax.shard_map(
        functools.partial(on_device, mesh.shape["prow"], mesh.shape["pcol"]),
        mesh=mesh,
        in_specs=placed,
        out_specs=(
            P("prow", "pcol"),
            P("pcol", None, None),
            P("prow", "pcol"),
            P("pcol", None, None),
            P("pcol", None, None),
        ),
        check_vma=False,
    )
```

```python
import functools

import jax
import jax.numpy as jnp
from jax import lax
from jax.experimental import pallas as pl
from jax.experimental.pallas import tpu as pltpu
from jax.sharding import PartitionSpec as P

KIDS = 2
PIECES = 8
MESH = pl.DeviceIdType.MESH


def gather_kernel(line, chips, tile_ref, low_ref, sig_ref, all_ref, s_self, y_send, y_recv, c_send,
                  c_recv, z_send, z_recv, w_send, w_recv, x_send, x_recv):
    row = lax.axis_index("prow")
    col = lax.axis_index("pcol")
    place, side = row // 2, row % 2
    chip, core = col // 2, col % 2
    height, width = tile_ref.shape
    depth = low_ref.shape[0]
    after, before = (place + 1) % line, (place + line - 1) % line
    dev_x = (place * 2 + 1 - side, col)
    dev_up = (after * 2 + side, col)
    dev_down = (before * 2 + side, col)
    dev_core = (row, chip * 2 + 1 - core)
    dev_y = [(row, (chip + d) % chips * 2 + core) for d in range(1, chips)]

    barrier = pltpu.get_barrier_semaphore()
    for dev in [dev_x, dev_up, dev_down, dev_core] + dev_y:
        pl.semaphore_signal(barrier, inc=1, device_id=dev, device_id_type=MESH)
    pl.semaphore_wait(barrier, 4 + len(dev_y))

    hs = height // PIECES
    ds = depth // PIECES

    def sig_at(owner, s):
        start = pl.multiple_of(owner * width, width)
        return sig_ref.at[pl.ds(s * hs, hs), pl.ds(start, width)]

    def low_at(block, s):
        start = pl.multiple_of(block * depth + s * ds, ds)
        return all_ref.at[pl.ds(start, ds), :]

    def remote(src, dst, send, recv, dev):
        return pltpu.make_async_remote_copy(src_ref=src, dst_ref=dst, send_sem=send,
                                            recv_sem=recv, device_id=dev, device_id_type=MESH)

    def tile_piece(s):
        return tile_ref.at[pl.ds(s * hs, hs), :]

    def low_piece(s):
        return low_ref.at[pl.ds(s * ds, ds), :]

    def to_x(slot, block, s, src):
        return remote(src, low_at(block, s), x_send.at[slot, s], x_recv.at[slot, s], dev_x)

    def to_z(way, t, block, s, src):
        return remote(src, low_at(block, s), z_send.at[way, t, s], z_recv.at[way, t, s],
                      dev_up if way == 0 else dev_down)

    def to_w(way, t, block):
        piece = low_at(block, 0)
        return remote(piece, piece, w_send.at[way, t], w_recv.at[way, t],
                      dev_up if way == 0 else dev_down)

    def to_y(d, s):
        return remote(tile_piece(s), sig_at(col, s), y_send.at[d - 1, s], y_recv.at[d - 1, s],
                      dev_y[d - 1])

    def to_core(d, s, owner, src):
        return remote(src, sig_at(owner, s), c_send.at[d, s], c_recv.at[d, s], dev_core)

    can_up = place < line - 1
    can_down = place > 0
    other = row + 1 - 2 * side
    for s in range(PIECES):
        to_x(0, row, s, low_piece(s)).start()
        pl.when(can_up)(lambda: to_z(0, 0, row, s, low_piece(s)).start())
        pl.when(can_down)(lambda: to_z(1, 0, row, s, low_piece(s)).start())
        for d in range(1, chips):
            to_y(d, s).start()
        to_core(0, s, col, tile_piece(s)).start()
    own_sig = pltpu.make_async_copy(
        tile_ref, sig_ref.at[:, pl.ds(pl.multiple_of(col * width, width), width)], s_self.at[0])
    own_low = pltpu.make_async_copy(
        low_ref, all_ref.at[pl.ds(pl.multiple_of(row * depth, depth), depth), :], s_self.at[1])
    own_sig.start()
    own_low.start()

    def from_line(way, t):
        block = row - 2 * t if way == 0 else row + 2 * t
        here = place - t >= 0 if way == 0 else place + t < line
        onward = (here & can_up) if way == 0 else (here & can_down)
        slot = t if way == 0 else line - 1 + t
        return block, here, onward, slot

    def pass_low(way, t, s):
        block, here, onward, slot = from_line(way, t)

        @pl.when(here)
        def _():
            to_z(way, t - 1, block, s, low_at(block, s)).wait_recv()
            if s > 0:
                to_x(slot, block, s, low_at(block, s)).start()
        if t < line - 1:
            @pl.when(onward)
            def _():
                to_z(way, t, block, s, low_at(block, s)).start()
        if s == 1:
            beside = block + other - row

            @pl.when(here)
            def _():
                to_w(way, t - 1, beside).wait_recv()
            if t < line - 1:
                @pl.when(onward)
                def _():
                    to_w(way, t, beside).start()

    def pass_sig(d, s):
        owner = (chip + chips - d) % chips * 2 + core
        to_y(d, s).wait_recv()
        to_core(d, s, owner, sig_at(owner, s)).start()

    lows = [(t, s) for t in range(1, line) for s in range(PIECES)]
    sigs = [(d, s) for s in range(PIECES) for d in range(1, chips)]
    to_x(0, row, 0, low_piece(0)).wait_recv()
    pl.when(can_up)(lambda: to_w(0, 0, other).start())
    pl.when(can_down)(lambda: to_w(1, 0, other).start())
    done = 0
    for i, (t, s) in enumerate(lows):
        pass_low(0, t, s)
        pass_low(1, t, s)
        upto = (i + 1) * len(sigs) // len(lows)
        for d, p in sigs[done:upto]:
            pass_sig(d, p)
        done = upto

    for s in range(PIECES):
        if s > 0:
            to_x(0, row, s, low_piece(s)).wait()
        else:
            to_x(0, row, s, low_piece(s)).wait_send()
            pl.when(can_up)(lambda: to_w(0, 0, other).wait_send())
            pl.when(can_down)(lambda: to_w(1, 0, other).wait_send())
        for d in range(chips):
            to_core(d, s, col, tile_piece(s)).wait()
        for d in range(1, chips):
            to_y(d, s).wait_send()
        pl.when(can_up)(lambda: to_z(0, 0, row, s, low_piece(s)).wait_send())
        pl.when(can_down)(lambda: to_z(1, 0, row, s, low_piece(s)).wait_send())
        for t in range(1, line):
            for way in range(2):
                block, here, onward, slot = from_line(way, t)

                if s > 0:
                    @pl.when(here)
                    def _():
                        to_x(slot, block, s, low_at(block, s)).wait()
                if t < line - 1:
                    @pl.when(onward)
                    def _():
                        to_z(way, t, block, s, low_at(block, s)).wait_send()
                        if s == 0:
                            to_w(way, t, block + other - row).wait_send()
    own_sig.wait()
    own_low.wait()


def gather_all(rows, cols, tile, low):
    line, chips = rows // 2, cols // 2
    height, width = tile.shape
    depth, count = low.shape
    dma = pltpu.SemaphoreType.DMA
    return pl.pallas_call(
        functools.partial(gather_kernel, line, chips),
        out_shape=(
            jax.ShapeDtypeStruct((height, cols * width), tile.dtype),
            jax.ShapeDtypeStruct((rows * depth, count), low.dtype),
        ),
        in_specs=[pl.BlockSpec(memory_space=pl.ANY)] * 2,
        out_specs=[pl.BlockSpec(memory_space=pl.ANY)] * 2,
        scratch_shapes=[
            dma((2,)),
            dma((max(chips - 1, 1), PIECES)), dma((max(chips - 1, 1), PIECES)),
            dma((chips, PIECES)), dma((chips, PIECES)),
            dma((2, line, PIECES)), dma((2, line, PIECES)),
            dma((2, line)), dma((2, line)),
            dma((2 * line - 1, PIECES)), dma((2 * line - 1, PIECES)),
        ],
        compiler_params=pltpu.CompilerParams(collective_id=0, has_side_effects=True),
    )(tile, low)


def sweep_kernel(par_here, sig_ref, low_ref, own_ref, keep_ref, link_ref, par_ref, kid_ref,
                 part_ref, acc):
    step = pl.program_id(0)
    width = link_ref.shape[1]
    kid_here = link_ref.shape[0]
    prod = jnp.dot(sig_ref[...], low_ref[...], preferred_element_type=jnp.float32)

    @pl.when(step == 0)
    def _():
        acc[...] = jnp.zeros_like(acc)

    def span(block):
        return slice(block * width, (block + 1) * width)

    def rows_dot(left, right):
        return lax.dot_general(left, right, (((0,), (0,)), ((), ())),
                               preferred_element_type=jnp.float32)

    for p in range(par_here):
        keep = keep_ref[:, span(p)].astype(jnp.float32)
        sig_par = (-prod[:, span(p)] * keep).astype(jnp.bfloat16)
        par_ref[:, span(p)] = sig_par
        acc[p] += rows_dot(own_ref[:, span(p)], sig_par)
        for c in range(p * KIDS, (p + 1) * KIDS):
            at = span(par_here + c)
            low = own_ref[:, at]
            carried = jnp.dot(sig_par, link_ref[c], preferred_element_type=jnp.float32)
            sig_kid = -(prod[:, at] + carried) * keep_ref[:, at].astype(jnp.float32)
            sig_kid = sig_kid.astype(jnp.bfloat16)
            kid_ref[:, span(c)] = sig_kid
            acc[par_here + c] += rows_dot(sig_par, low)
            acc[par_here + kid_here + c] += rows_dot(low, sig_kid)

    @pl.when(step == pl.num_programs(0) - 1)
    def _():
        part_ref[...] = acc[...].astype(part_ref.dtype)


def sweep(par_here, sigma_rows, low_rows, own, keep, link):
    kid_here, width, _ = link.shape
    height, order = sigma_rows.shape
    count = own.shape[1]
    blocks = par_here + 2 * kid_here

    def by_row(columns):
        return pl.BlockSpec((width, columns), lambda i: (i, 0))

    return pl.pallas_call(
        functools.partial(sweep_kernel, par_here),
        grid=(height // width,),
        out_shape=(
            jax.ShapeDtypeStruct((height, par_here * width), jnp.bfloat16),
            jax.ShapeDtypeStruct((height, kid_here * width), jnp.bfloat16),
            jax.ShapeDtypeStruct((blocks, width, width), jnp.bfloat16),
        ),
        in_specs=[
            by_row(order),
            pl.BlockSpec((order, count), lambda i: (0, 0)),
            by_row(count),
            by_row(count),
            pl.BlockSpec(link.shape, lambda i: (0, 0, 0)),
        ],
        out_specs=[
            by_row(par_here * width),
            by_row(kid_here * width),
            pl.BlockSpec((blocks, width, width), lambda i: (0, 0, 0)),
        ],
        scratch_shapes=[pltpu.VMEM((blocks, width, width), jnp.float32)],
        compiler_params=pltpu.CompilerParams(vmem_limit_bytes=56 * 1024 * 1024),
    )(sigma_rows, low_rows, own, keep, link)


def sum_kernel(count, part_ref, out_ref, got, s_send, s_recv, g_send, g_recv):
    row = lax.axis_index("prow")
    col = lax.axis_index("pcol")
    size = part_ref.shape[0] // count
    peers = [((row + d) % count, col) for d in range(1, count)]
    barrier = pltpu.get_barrier_semaphore()
    for dev in peers:
        pl.semaphore_signal(barrier, inc=1, device_id=dev, device_id_type=MESH)
    pl.semaphore_wait(barrier, len(peers))

    def share(block):
        return pl.ds(pl.multiple_of(block * size, size), size)

    def scatter(d):
        return pltpu.make_async_remote_copy(
            src_ref=part_ref.at[share((row + d) % count), :], dst_ref=got.at[d - 1],
            send_sem=s_send.at[d - 1], recv_sem=s_recv.at[d - 1], device_id=peers[d - 1],
            device_id_type=MESH)

    def spread(d):
        return pltpu.make_async_remote_copy(
            src_ref=out_ref.at[share(row), :], dst_ref=out_ref.at[share(row), :],
            send_sem=g_send.at[d - 1], recv_sem=g_recv.at[d - 1], device_id=peers[d - 1],
            device_id_type=MESH)

    for d in range(1, count):
        scatter(d).start()
    total = part_ref[share(row), :].astype(jnp.float32)
    for d in range(1, count):
        scatter(d).wait_recv()
        total = total + got[d - 1].astype(jnp.float32)
    out_ref[share(row), :] = total.astype(out_ref.dtype)
    for d in range(1, count):
        spread(d).start()
    for d in range(1, count):
        scatter(d).wait_send()
        spread(d).wait()


def sum_parts(count, parts):
    size = parts.shape[0] // count
    dma = pltpu.SemaphoreType.DMA
    return pl.pallas_call(
        functools.partial(sum_kernel, count),
        out_shape=jax.ShapeDtypeStruct(parts.shape, parts.dtype),
        in_specs=[pl.BlockSpec(memory_space=pltpu.VMEM)],
        out_specs=pl.BlockSpec(memory_space=pltpu.VMEM),
        scratch_shapes=[
            pltpu.VMEM((count - 1, size, parts.shape[1]), parts.dtype),
            dma((count - 1,)), dma((count - 1,)), dma((count - 1,)), dma((count - 1,)),
        ],
        compiler_params=pltpu.CompilerParams(collective_id=1, has_side_effects=True),
    )(parts)


def expand_rows(mask, width):
    count, blocks = mask.shape
    spread = jnp.broadcast_to(
        mask.T.astype(jnp.float32)[:, None, :, None], (blocks, width, count, width)
    )
    return spread.reshape(blocks * width, count * width)


def batch_mult(left, right):
    return jnp.einsum("cab,cbd->cad", left, right, precision=lax.Precision.HIGHEST)


def batch_tmult(left, right):
    return jnp.einsum("cba,cbd->cad", left, right, precision=lax.Precision.HIGHEST)


def on_device(rows, cols, sigma_top, panel_par, panel_kid, link_kid, dinv_par, dinv_kid, mask_par, mask_kid):
    width = dinv_par.shape[1]
    par_here = dinv_par.shape[0]
    kid_here = dinv_kid.shape[0]
    kid_pattern = mask_kid * jnp.repeat(mask_par, KIDS, axis=0)
    keep = jnp.concatenate(
        [expand_rows(mask_par, width), expand_rows(kid_pattern, width)], axis=1
    ).astype(jnp.bfloat16)
    low_own = jnp.concatenate([panel_par, panel_kid], axis=1) * keep
    sigma_rows, low_rows = gather_all(rows, cols, sigma_top, low_own)
    sigma_par, sigma_kid, parts = sweep(par_here, sigma_rows, low_rows, low_own, keep, link_kid)
    link_wide = link_kid.astype(jnp.float32)
    total = sum_parts(rows, parts.reshape(-1, width)).astype(jnp.float32)
    total = total.reshape(parts.shape)
    sum_par = total[:par_here]
    cross_sum = total[par_here : par_here + kid_here]
    kid_sum = total[par_here + kid_here :]
    diag_par = dinv_par - sum_par
    diag_spread = jnp.repeat(diag_par, KIDS, axis=0)
    link_sigma = -(cross_sum + batch_mult(diag_spread, link_wide))
    diag_kid = dinv_kid - kid_sum - batch_tmult(link_wide, link_sigma)
    return (sigma_par, diag_par, sigma_kid, link_sigma, diag_kid)


def solution(mesh):
    placed = (
        P("prow", "pcol"),
        P("prow", "pcol"),
        P("prow", "pcol"),
        P("pcol", None, None),
        P("pcol", None, None),
        P("pcol", None, None),
        P("pcol", "prow"),
        P("pcol", "prow"),
    )
    return jax.shard_map(
        functools.partial(on_device, mesh.shape["prow"], mesh.shape["pcol"]),
        mesh=mesh,
        in_specs=placed,
        out_specs=(
            P("prow", "pcol"),
            P("pcol", None, None),
            P("prow", "pcol"),
            P("pcol", None, None),
            P("pcol", None, None),
        ),
        check_vma=False,
    )
```

```python
import functools

import jax
import jax.numpy as jnp
from jax import lax
from jax.experimental import pallas as pl
from jax.experimental.pallas import tpu as pltpu
from jax.sharding import PartitionSpec as P

KIDS = 2
PIECES = 16
MESH = pl.DeviceIdType.MESH


def gather_kernel(line, chips, tile_ref, low_ref, sig_ref, all_ref, s_self, y_send, y_recv, c_send,
                  c_recv, z_send, z_recv, w_send, w_recv, x_send, x_recv):
    row = lax.axis_index("prow")
    col = lax.axis_index("pcol")
    place, side = row // 2, row % 2
    chip, core = col // 2, col % 2
    height, width = tile_ref.shape
    depth = low_ref.shape[0]
    after, before = (place + 1) % line, (place + line - 1) % line
    dev_x = (place * 2 + 1 - side, col)
    dev_up = (after * 2 + side, col)
    dev_down = (before * 2 + side, col)
    dev_core = (row, chip * 2 + 1 - core)
    dev_y = [(row, (chip + d) % chips * 2 + core) for d in range(1, chips)]

    barrier = pltpu.get_barrier_semaphore()
    for dev in [dev_x, dev_up, dev_down, dev_core] + dev_y:
        pl.semaphore_signal(barrier, inc=1, device_id=dev, device_id_type=MESH)
    pl.semaphore_wait(barrier, 4 + len(dev_y))

    hs = height // PIECES
    ds = depth // PIECES

    def sig_at(owner, s):
        start = pl.multiple_of(owner * width, width)
        return sig_ref.at[pl.ds(s * hs, hs), pl.ds(start, width)]

    def low_at(block, s):
        start = pl.multiple_of(block * depth + s * ds, ds)
        return all_ref.at[pl.ds(start, ds), :]

    def remote(src, dst, send, recv, dev):
        return pltpu.make_async_remote_copy(src_ref=src, dst_ref=dst, send_sem=send,
                                            recv_sem=recv, device_id=dev, device_id_type=MESH)

    def tile_piece(s):
        return tile_ref.at[pl.ds(s * hs, hs), :]

    def low_piece(s):
        return low_ref.at[pl.ds(s * ds, ds), :]

    def to_x(slot, block, s, src):
        return remote(src, low_at(block, s), x_send.at[slot, s], x_recv.at[slot, s], dev_x)

    def to_z(way, t, block, s, src):
        return remote(src, low_at(block, s), z_send.at[way, t, s], z_recv.at[way, t, s],
                      dev_up if way == 0 else dev_down)

    def to_w(way, t, block):
        piece = low_at(block, 0)
        return remote(piece, piece, w_send.at[way, t], w_recv.at[way, t],
                      dev_up if way == 0 else dev_down)

    def to_y(d, s):
        return remote(tile_piece(s), sig_at(col, s), y_send.at[d - 1, s], y_recv.at[d - 1, s],
                      dev_y[d - 1])

    def to_core(d, s, owner, src):
        return remote(src, sig_at(owner, s), c_send.at[d, s], c_recv.at[d, s], dev_core)

    can_up = place < line - 1
    can_down = place > 0
    other = row + 1 - 2 * side
    for s in range(PIECES):
        to_x(0, row, s, low_piece(s)).start()
        pl.when(can_up)(lambda: to_z(0, 0, row, s, low_piece(s)).start())
        pl.when(can_down)(lambda: to_z(1, 0, row, s, low_piece(s)).start())
        for d in range(1, chips):
            to_y(d, s).start()
        to_core(0, s, col, tile_piece(s)).start()
    own_sig = pltpu.make_async_copy(
        tile_ref, sig_ref.at[:, pl.ds(pl.multiple_of(col * width, width), width)], s_self.at[0])
    own_low = pltpu.make_async_copy(
        low_ref, all_ref.at[pl.ds(pl.multiple_of(row * depth, depth), depth), :], s_self.at[1])
    own_sig.start()
    own_low.start()

    def from_line(way, t):
        block = row - 2 * t if way == 0 else row + 2 * t
        here = place - t >= 0 if way == 0 else place + t < line
        onward = (here & can_up) if way == 0 else (here & can_down)
        slot = t if way == 0 else line - 1 + t
        return block, here, onward, slot

    def pass_low(way, t, s):
        block, here, onward, slot = from_line(way, t)

        @pl.when(here)
        def _():
            to_z(way, t - 1, block, s, low_at(block, s)).wait_recv()
            if s > 0:
                to_x(slot, block, s, low_at(block, s)).start()
        if t < line - 1:
            @pl.when(onward)
            def _():
                to_z(way, t, block, s, low_at(block, s)).start()
        if s == 1:
            beside = block + other - row

            @pl.when(here)
            def _():
                to_w(way, t - 1, beside).wait_recv()
            if t < line - 1:
                @pl.when(onward)
                def _():
                    to_w(way, t, beside).start()

    def pass_sig(d, s):
        owner = (chip + chips - d) % chips * 2 + core
        to_y(d, s).wait_recv()
        to_core(d, s, owner, sig_at(owner, s)).start()

    lows = [(t, s) for t in range(1, line) for s in range(PIECES)]
    sigs = [(d, s) for s in range(PIECES) for d in range(1, chips)]
    to_x(0, row, 0, low_piece(0)).wait_recv()
    pl.when(can_up)(lambda: to_w(0, 0, other).start())
    pl.when(can_down)(lambda: to_w(1, 0, other).start())
    done = 0
    for i, (t, s) in enumerate(lows):
        pass_low(0, t, s)
        pass_low(1, t, s)
        upto = (i + 1) * len(sigs) // len(lows)
        for d, p in sigs[done:upto]:
            pass_sig(d, p)
        done = upto

    for s in range(PIECES):
        if s > 0:
            to_x(0, row, s, low_piece(s)).wait()
        else:
            to_x(0, row, s, low_piece(s)).wait_send()
            pl.when(can_up)(lambda: to_w(0, 0, other).wait_send())
            pl.when(can_down)(lambda: to_w(1, 0, other).wait_send())
        for d in range(chips):
            to_core(d, s, col, tile_piece(s)).wait()
        for d in range(1, chips):
            to_y(d, s).wait_send()
        pl.when(can_up)(lambda: to_z(0, 0, row, s, low_piece(s)).wait_send())
        pl.when(can_down)(lambda: to_z(1, 0, row, s, low_piece(s)).wait_send())
        for t in range(1, line):
            for way in range(2):
                block, here, onward, slot = from_line(way, t)

                if s > 0:
                    @pl.when(here)
                    def _():
                        to_x(slot, block, s, low_at(block, s)).wait()
                if t < line - 1:
                    @pl.when(onward)
                    def _():
                        to_z(way, t, block, s, low_at(block, s)).wait_send()
                        if s == 0:
                            to_w(way, t, block + other - row).wait_send()
    own_sig.wait()
    own_low.wait()


def gather_all(rows, cols, tile, low):
    line, chips = rows // 2, cols // 2
    height, width = tile.shape
    depth, count = low.shape
    dma = pltpu.SemaphoreType.DMA
    return pl.pallas_call(
        functools.partial(gather_kernel, line, chips),
        out_shape=(
            jax.ShapeDtypeStruct((height, cols * width), tile.dtype),
            jax.ShapeDtypeStruct((rows * depth, count), low.dtype),
        ),
        in_specs=[pl.BlockSpec(memory_space=pl.ANY)] * 2,
        out_specs=[pl.BlockSpec(memory_space=pl.ANY)] * 2,
        scratch_shapes=[
            dma((2,)),
            dma((max(chips - 1, 1), PIECES)), dma((max(chips - 1, 1), PIECES)),
            dma((chips, PIECES)), dma((chips, PIECES)),
            dma((2, line, PIECES)), dma((2, line, PIECES)),
            dma((2, line)), dma((2, line)),
            dma((2 * line - 1, PIECES)), dma((2 * line - 1, PIECES)),
        ],
        compiler_params=pltpu.CompilerParams(collective_id=0, has_side_effects=True),
    )(tile, low)


def sweep_kernel(par_here, sig_ref, low_ref, own_ref, keep_ref, link_ref, par_ref, kid_ref,
                 part_ref, acc):
    step = pl.program_id(0)
    width = link_ref.shape[1]
    kid_here = link_ref.shape[0]
    prod = jnp.dot(sig_ref[...], low_ref[...], preferred_element_type=jnp.float32)

    @pl.when(step == 0)
    def _():
        acc[...] = jnp.zeros_like(acc)

    def span(block):
        return slice(block * width, (block + 1) * width)

    def rows_dot(left, right):
        return lax.dot_general(left, right, (((0,), (0,)), ((), ())),
                               preferred_element_type=jnp.float32)

    for p in range(par_here):
        keep = keep_ref[:, span(p)].astype(jnp.float32)
        sig_par = (-prod[:, span(p)] * keep).astype(jnp.bfloat16)
        par_ref[:, span(p)] = sig_par
        acc[p] += rows_dot(own_ref[:, span(p)], sig_par)
        for c in range(p * KIDS, (p + 1) * KIDS):
            at = span(par_here + c)
            low = own_ref[:, at]
            carried = jnp.dot(sig_par, link_ref[c], preferred_element_type=jnp.float32)
            sig_kid = -(prod[:, at] + carried) * keep_ref[:, at].astype(jnp.float32)
            sig_kid = sig_kid.astype(jnp.bfloat16)
            kid_ref[:, span(c)] = sig_kid
            acc[par_here + c] += rows_dot(sig_par, low)
            acc[par_here + kid_here + c] += rows_dot(low, sig_kid)

    @pl.when(step == pl.num_programs(0) - 1)
    def _():
        part_ref[...] = acc[...].astype(part_ref.dtype)


def sweep(par_here, sigma_rows, low_rows, own, keep, link):
    kid_here, width, _ = link.shape
    height, order = sigma_rows.shape
    count = own.shape[1]
    blocks = par_here + 2 * kid_here

    def by_row(columns):
        return pl.BlockSpec((width, columns), lambda i: (i, 0))

    return pl.pallas_call(
        functools.partial(sweep_kernel, par_here),
        grid=(height // width,),
        out_shape=(
            jax.ShapeDtypeStruct((height, par_here * width), jnp.bfloat16),
            jax.ShapeDtypeStruct((height, kid_here * width), jnp.bfloat16),
            jax.ShapeDtypeStruct((blocks, width, width), jnp.bfloat16),
        ),
        in_specs=[
            by_row(order),
            pl.BlockSpec((order, count), lambda i: (0, 0)),
            by_row(count),
            by_row(count),
            pl.BlockSpec(link.shape, lambda i: (0, 0, 0)),
        ],
        out_specs=[
            by_row(par_here * width),
            by_row(kid_here * width),
            pl.BlockSpec((blocks, width, width), lambda i: (0, 0, 0)),
        ],
        scratch_shapes=[pltpu.VMEM((blocks, width, width), jnp.float32)],
        compiler_params=pltpu.CompilerParams(vmem_limit_bytes=56 * 1024 * 1024),
    )(sigma_rows, low_rows, own, keep, link)


def sum_kernel(count, part_ref, out_ref, got, s_send, s_recv, g_send, g_recv):
    row = lax.axis_index("prow")
    col = lax.axis_index("pcol")
    size = part_ref.shape[0] // count
    peers = [((row + d) % count, col) for d in range(1, count)]
    barrier = pltpu.get_barrier_semaphore()
    for dev in peers:
        pl.semaphore_signal(barrier, inc=1, device_id=dev, device_id_type=MESH)
    pl.semaphore_wait(barrier, len(peers))

    def share(block):
        return pl.ds(pl.multiple_of(block * size, size), size)

    def scatter(d):
        return pltpu.make_async_remote_copy(
            src_ref=part_ref.at[share((row + d) % count), :], dst_ref=got.at[d - 1],
            send_sem=s_send.at[d - 1], recv_sem=s_recv.at[d - 1], device_id=peers[d - 1],
            device_id_type=MESH)

    def spread(d):
        return pltpu.make_async_remote_copy(
            src_ref=out_ref.at[share(row), :], dst_ref=out_ref.at[share(row), :],
            send_sem=g_send.at[d - 1], recv_sem=g_recv.at[d - 1], device_id=peers[d - 1],
            device_id_type=MESH)

    for d in range(1, count):
        scatter(d).start()
    total = part_ref[share(row), :].astype(jnp.float32)
    for d in range(1, count):
        scatter(d).wait_recv()
        total = total + got[d - 1].astype(jnp.float32)
    out_ref[share(row), :] = total.astype(out_ref.dtype)
    for d in range(1, count):
        spread(d).start()
    for d in range(1, count):
        scatter(d).wait_send()
        spread(d).wait()


def sum_parts(count, parts):
    size = parts.shape[0] // count
    dma = pltpu.SemaphoreType.DMA
    return pl.pallas_call(
        functools.partial(sum_kernel, count),
        out_shape=jax.ShapeDtypeStruct(parts.shape, parts.dtype),
        in_specs=[pl.BlockSpec(memory_space=pltpu.VMEM)],
        out_specs=pl.BlockSpec(memory_space=pltpu.VMEM),
        scratch_shapes=[
            pltpu.VMEM((count - 1, size, parts.shape[1]), parts.dtype),
            dma((count - 1,)), dma((count - 1,)), dma((count - 1,)), dma((count - 1,)),
        ],
        compiler_params=pltpu.CompilerParams(collective_id=1, has_side_effects=True),
    )(parts)


def expand_rows(mask, width):
    count, blocks = mask.shape
    spread = jnp.broadcast_to(
        mask.T.astype(jnp.float32)[:, None, :, None], (blocks, width, count, width)
    )
    return spread.reshape(blocks * width, count * width)


def batch_mult(left, right):
    return jnp.einsum("cab,cbd->cad", left, right, precision=lax.Precision.HIGHEST)


def batch_tmult(left, right):
    return jnp.einsum("cba,cbd->cad", left, right, precision=lax.Precision.HIGHEST)


def on_device(rows, cols, sigma_top, panel_par, panel_kid, link_kid, dinv_par, dinv_kid, mask_par, mask_kid):
    width = dinv_par.shape[1]
    par_here = dinv_par.shape[0]
    kid_here = dinv_kid.shape[0]
    kid_pattern = mask_kid * jnp.repeat(mask_par, KIDS, axis=0)
    keep = jnp.concatenate(
        [expand_rows(mask_par, width), expand_rows(kid_pattern, width)], axis=1
    ).astype(jnp.bfloat16)
    low_own = jnp.concatenate([panel_par, panel_kid], axis=1) * keep
    sigma_rows, low_rows = gather_all(rows, cols, sigma_top, low_own)
    sigma_par, sigma_kid, parts = sweep(par_here, sigma_rows, low_rows, low_own, keep, link_kid)
    link_wide = link_kid.astype(jnp.float32)
    total = sum_parts(rows, parts.reshape(-1, width)).astype(jnp.float32)
    total = total.reshape(parts.shape)
    sum_par = total[:par_here]
    cross_sum = total[par_here : par_here + kid_here]
    kid_sum = total[par_here + kid_here :]
    diag_par = dinv_par - sum_par
    diag_spread = jnp.repeat(diag_par, KIDS, axis=0)
    link_sigma = -(cross_sum + batch_mult(diag_spread, link_wide))
    diag_kid = dinv_kid - kid_sum - batch_tmult(link_wide, link_sigma)
    return (sigma_par, diag_par, sigma_kid, link_sigma, diag_kid)


def solution(mesh):
    placed = (
        P("prow", "pcol"),
        P("prow", "pcol"),
        P("prow", "pcol"),
        P("pcol", None, None),
        P("pcol", None, None),
        P("pcol", None, None),
        P("pcol", "prow"),
        P("pcol", "prow"),
    )
    return jax.shard_map(
        functools.partial(on_device, mesh.shape["prow"], mesh.shape["pcol"]),
        mesh=mesh,
        in_specs=placed,
        out_specs=(
            P("prow", "pcol"),
            P("pcol", None, None),
            P("prow", "pcol"),
            P("pcol", None, None),
            P("pcol", None, None),
        ),
        check_vma=False,
    )
```
